32 devices in a mesh: gz: 8 (over z, y), gy: 4 (over x, core).
Axes of the slice: x: 2, y: 2, z: 4, core: 2. Of those that a mesh axis runs over, the one named last changes fastest.
Arguments:
- concentration: float32 [128, 32, 128], P('gz', 'gy'), may hold values from 0 to 2
- phases: int32 [128, 32, 128], P('gz', 'gy'), may hold values from 0 to 2, as said below
- grains: int32 [128, 32, 128], P('gz', 'gy'), may hold values from 0 to 63, as said below
- grain_class: int32 [64], replicated, may hold values from 0 to 3
- diffusivity: float32 [3, 4], replicated, may hold values from 1 to 2000
Outputs:
- solution: float32 [128, 32, 128], P('gz', 'gy')
The draws below stay inside these ranges and needn't reach their ends.
Inputs may be any that keep to these rules, and one draw needn't show every extreme that they name: `phases`: constant on aligned blocks of 8 x 8 x 8 cells. `grains`: constant on aligned blocks of 4 x 4 x 4 cells.
All inputs are finite; a program needn't handle non-finite values.
Results may differ from the reference program's by a relative error of at most 0.0003.
Values sent between devices are 32-bit elements; how exact they have to be, the bound alone decides.
A program may use at most 64 MiB of HBM per device.

```python
import math
import jax
import jax.numpy as jnp
from jax import lax

NX = 128
NPH = 3
NCLS = 4
NGRAIN = 64
CYCLES = 2
COARSE = 6
NZ = 128
NY = 32


def draw_concentration(key, part):
    own_key = jax.random.fold_in(key, 11)
    rough = jax.random.uniform(own_key, (NZ, NY, NX), jnp.float32, -1.0, 1.0)
    return 1.0 + 0.8 * rough


def draw_phases(key, part):
    own_key = jax.random.fold_in(key, 23)
    coarse = jax.random.randint(own_key, (NZ // 8, NY // 8, NX // 8), 0, NPH)
    return jnp.repeat(jnp.repeat(jnp.repeat(coarse, 8, 0), 8, 1), 8, 2).astype(jnp.int32)


def draw_grains(key, part):
    own_key = jax.random.fold_in(key, 37)
    coarse = jax.random.randint(own_key, (NZ // 4, NY // 4, NX // 4), 0, NGRAIN)
    return jnp.repeat(jnp.repeat(jnp.repeat(coarse, 4, 0), 4, 1), 4, 2).astype(jnp.int32)


def with_ends(drawn, key, smallest, largest):
    dims = drawn.shape
    index_at = [jax.random.randint(jax.random.fold_in(key, axis), (), 0, dims[axis]) for axis in range(len(dims))]
    drawn = drawn.at[tuple(index_at)].set(smallest)
    longest = dims.index(max(dims))
    index_at[longest] = (index_at[longest] + 1) % dims[longest]
    return drawn.at[tuple(index_at)].set(largest)


def setup_inputs(seed: int = 0) -> dict:
    key_list = jax.random.split(jax.random.key(seed), 6)
    return {
        "concentration": draw_concentration(jax.random.fold_in(key_list[5], 71), 0),
        "phases": draw_phases(jax.random.fold_in(key_list[5], 71), 0),
        "grains": draw_grains(jax.random.fold_in(key_list[5], 71), 0),
        "grain_class": with_ends(jax.random.randint(key_list[3], (NGRAIN,), 0, NCLS), jax.random.fold_in(key_list[3], 1), 0, NCLS - 1).astype(jnp.int32),
        "diffusivity": jnp.clip(jnp.exp(jax.random.uniform(key_list[4], (NPH, NCLS), jnp.float32, math.log(1.0), math.log(2000.0))), 1.0, 2000.0),
    }


RELAX_WEIGHT = 0.8


def harmonic(near_k, far_k):
    return 2.0 * near_k * far_k / (near_k + far_k)


def face_set(padded, margin, y_start, y_total):
    centre = padded[1:-1, 1:-1]
    row_index = lax.broadcasted_iota(jnp.int32, centre.shape, 1) + y_start - margin
    col_index = lax.broadcasted_iota(jnp.int32, centre.shape, 2)
    z_low = harmonic(centre, padded[:-2, 1:-1])
    z_high = harmonic(centre, padded[2:, 1:-1])
    y_low = jnp.where(row_index == 0, 0.0, harmonic(centre, padded[1:-1, :-2]))
    y_high = jnp.where(row_index == y_total - 1, 0.0, harmonic(centre, padded[1:-1, 2:]))
    x_low = jnp.where(col_index == 0, 0.0, harmonic(centre, jnp.roll(centre, 1, 2)))
    x_high = jnp.where(col_index == centre.shape[2] - 1, 0.0, harmonic(centre, jnp.roll(centre, -1, 2)))
    diagonal = 1.0 + z_low + z_high + y_low + y_high + x_low + x_high
    return (z_low, z_high, y_low, y_high, x_low, x_high, diagonal)


def apply_operator(padded, faces):
    z_low, z_high, y_low, y_high, x_low, x_high, diagonal = faces
    centre = padded[1:-1, 1:-1]
    coupled = (z_low * padded[:-2, 1:-1] + z_high * padded[2:, 1:-1]
               + y_low * padded[1:-1, :-2] + y_high * padded[1:-1, 2:]
               + x_low * jnp.roll(centre, 1, 2) + x_high * jnp.roll(centre, -1, 2))
    return centre, diagonal * centre - coupled


def relax_sweep(padded, source, faces):
    centre, image = apply_operator(padded, faces)
    return centre + RELAX_WEIGHT * (source - image) / faces[6]


def defect(padded, source, faces):
    return source - apply_operator(padded, faces)[1]


def restrict(values):
    extent = values.shape
    return values.reshape(extent[0] // 2, 2, extent[1] // 2, 2, extent[2] // 2, 2).mean(axis=(1, 3, 5))


def prolong(coarse):
    return jnp.repeat(jnp.repeat(jnp.repeat(coarse, 2, 0), 2, 1), 2, 2)


def pad_periodic(values):
    wrapped = jnp.concatenate([values[-1:], values, values[:1]], axis=0)
    return jnp.pad(wrapped, ((0, 0), (1, 1), (0, 0)), mode="edge")


def vcycle(level_index, field, source, faces_list):
    faces = faces_list[level_index]
    if level_index == len(faces_list) - 1:
        for _ in range(COARSE):
            field = relax_sweep(pad_periodic(field), source, faces)
        return field
    for _ in range(2):
        field = relax_sweep(pad_periodic(field), source, faces)
    residual = defect(pad_periodic(field), source, faces)
    coarse_source = restrict(residual)
    correction = vcycle(level_index + 1, jnp.zeros_like(coarse_source), coarse_source, faces_list)
    field = field + prolong(correction)
    for _ in range(2):
        field = relax_sweep(pad_periodic(field), source, faces)
    return field


def reference(concentration, phases, grains, grain_class, diffusivity):
    kappa = diffusivity[phases, grain_class[grains]]
    faces_list = []
    for level_index in range(5):
        if level_index > 0:
            kappa = 0.5 * restrict(kappa)
        faces_list.append(face_set(pad_periodic(kappa), 0, 0, kappa.shape[1]))
    field = jnp.zeros_like(concentration)
    for _ in range(CYCLES):
        field = vcycle(0, field, concentration, faces_list)
    return field
```

```python
import functools

import jax
import jax.numpy as jnp
from jax import lax
from jax.experimental import pallas as pl
from jax.experimental.pallas import tpu as pltpu
from jax.sharding import PartitionSpec as P

CYCLES = 2
COARSE = 6
RELAX_WEIGHT = 0.8
KEEP = 1.0 - RELAX_WEIGHT
BLOCK = 4
SIDE = 3
MESH = pl.DeviceIdType.MESH

XL, XH, YL, YH, ZL, ZH, KI, W0, WM, WL = range(10)


def roll(values, shift, axis):
    return pltpu.roll(values, shift % values.shape[axis], axis)


def harmonic(near_k, far_k):
    return 2.0 * near_k * far_k / (near_k + far_k)


def pair_sum(values, stride, axis):
    index = lax.broadcasted_iota(jnp.int32, values.shape, axis)
    odd = (index & stride) != 0
    other = jnp.where(odd, roll(values, stride, axis), roll(values, -stride, axis))
    return values + other


def block_sum(values, sy, sx):
    rows = values.shape[0]
    halved = jnp.concatenate(
        [values[j : j + 1] + values[j + 1 : j + 2] for j in range(0, rows, 2)], axis=0
    )
    return pair_sum(pair_sum(halved, sy, 1), sx, 2)


def doubled(values):
    rows = values.shape[0]
    return jnp.concatenate([values[j // 2 : j // 2 + 1] for j in range(2 * rows)], axis=0)


class Level:
    def __init__(self, faces, kappa, scale, blocks, rpb, u, sy, sx, periodic):
        self.faces, self.kappa, self.scale = faces, kappa, scale
        self.blocks, self.rpb, self.u = blocks, rpb, u
        self.sy, self.sx, self.periodic = sy, sx, periodic

    def loop(self, body, low=0, high=None):
        high = self.blocks if high is None else high

        def step(i, carry):
            body(i * self.u)
            return carry

        lax.fori_loop(low // self.u, high // self.u, step, 0)

    def ghosts(self, ref):
        if self.periodic:
            rows = self.blocks * self.rpb
            ref[0:1] = ref[rows : rows + 1]
            ref[rows + 1 : rows + 2] = ref[1:2]

    def build(self):
        faces, rpb, u = self.faces, self.rpb, self.u

        def body(b):
            k = self.kappa[pl.ds(b + 1, u)] * self.scale
            below = self.kappa[pl.ds(b, u)] * self.scale
            above = self.kappa[pl.ds(b + 2, u)] * self.scale
            row = lax.broadcasted_iota(jnp.int32, k.shape, 1)
            col = lax.broadcasted_iota(jnp.int32, k.shape, 2)
            y_size, x_size = k.shape[1], k.shape[2]
            sy, sx = self.sy, self.sx
            xl = jnp.where(col < sx, 0.0, harmonic(k, roll(k, sx, 2)))
            xh = jnp.where(col >= x_size - sx, 0.0, harmonic(k, roll(k, -sx, 2)))
            yl = jnp.where(row < sy, 0.0, harmonic(k, roll(k, sy, 1)))
            yh = jnp.where(row >= y_size - sy, 0.0, harmonic(k, roll(k, -sy, 1)))
            zl = harmonic(k, below)
            zh = harmonic(k, above)
            base = 1.0 + xl + xh + yl + yh
            at = pl.ds(b, u)
            for name, value in ((XL, xl), (XH, xh), (YL, yl), (YH, yh), (ZL, zl), (ZH, zh), (KI, k)):
                faces[name, at] = value
            if rpb == 1:
                faces[W0, at] = RELAX_WEIGHT / (base + zl + zh)
            else:
                faces[W0, at] = RELAX_WEIGHT / (base + zl + k)
                faces[WL, at] = RELAX_WEIGHT / (base + zh + k)
                if rpb > 2:
                    faces[WM, at] = RELAX_WEIGHT / (base + k + k)

        self.loop(body)

    def weight(self, b):
        at = pl.ds(b, self.u)
        if self.rpb == 1:
            return self.faces[W0, at]
        middle = [self.faces[WM, at]] * (self.rpb - 2) if self.rpb > 2 else []
        return jnp.concatenate([self.faces[W0, at], *middle, self.faces[WL, at]], axis=0)

    def z_faces(self, b):
        at = pl.ds(b, self.u)
        low, high = self.faces[ZL, at], self.faces[ZH, at]
        if self.rpb == 1:
            return low, high
        inner = [self.faces[KI, at]] * (self.rpb - 1)
        return jnp.concatenate([low, *inner], axis=0), jnp.concatenate([*inner, high], axis=0)

    def terms(self, src, b):
        n = self.u * self.rpb
        ext = src[pl.ds(b * self.rpb, n + 2)]
        centre = ext[1 : n + 1]
        at = pl.ds(b, self.u)
        low, high = self.z_faces(b)
        pairs = [
            (low, ext[:n]),
            (high, ext[2:]),
            (self.faces[YL, at], roll(centre, self.sy, 1)),
            (self.faces[YH, at], roll(centre, -self.sy, 1)),
            (self.faces[XL, at], roll(centre, self.sx, 2)),
            (self.faces[XH, at], roll(centre, -self.sx, 2)),
        ]
        return centre, pairs

    def rows(self, b, shift=0):
        return pl.ds(b * self.rpb + shift, self.u * self.rpb)

    def first(self, dst, source):
        def body(b):
            dst[self.rows(b, 1)] = self.weight(b) * source[self.rows(b)]

        self.loop(body)
        self.ghosts(dst)

    def relax(self, dst, src, source, low=0, high=None):
        def body(b):
            centre, pairs = self.terms(src, b)
            total = source[self.rows(b)]
            for face, value in pairs:
                total = total + face * value
            dst[self.rows(b, 1)] = KEEP * centre + self.weight(b) * total

        self.loop(body, low, high)
        self.ghosts(dst)

    def restricted(self, src, source, b):
        centre, pairs = self.terms(src, b)
        rest = source[self.rows(b)] - centre
        for face, value in pairs:
            rest = rest - face * (centre - value)
        return block_sum(rest, self.sy, self.sx) * 0.125

    def restrict(self, dst, src, source, low=0, high=None):
        half = self.u * self.rpb // 2

        def body(b):
            dst[pl.ds(b * self.rpb // 2, half)] = self.restricted(src, source, b)

        self.loop(body, low, high)

    def correct(self, dst, coarse, low=0, high=None):
        half = self.u * self.rpb // 2

        def body(b):
            fine = self.rows(b, 1)
            dst[fine] = dst[fine] + doubled(coarse[pl.ds(b * self.rpb // 2 + 1, half)])

        self.loop(body, low, high)
        self.ghosts(dst)


def kernel(
    gz, gy, conc, phases, grains, grain_class, diffusivity, out,
    c_all, k_all, va, vb, vn, g1, v1a, v1b, rest, spread,
    k2, g2, v2a, v2b, k3, g3, v3a, v3b, k4, g4, v4a, v4b, f0, f1, f2, f3, f4,
    c_send, c_recv, k_send, k_recv, k2_send, k2_recv, g2_send, g2_recv, v_send, v_recv,
):
    my_z, my_y = lax.axis_index("gz"), lax.axis_index("gy")
    z_len, y_len = conc.shape[0], conc.shape[1]
    own = z_len // BLOCK
    blocks = own + 2 * SIDE
    halo = SIDE * BLOCK
    nz2 = k2.shape[0] - 2
    y2 = k2.shape[1]
    zs = [lax.rem(my_z + o, gz) for o in range(gz)]
    ys = [lax.rem(my_y + o, gy) for o in range(gy)]

    barrier = pltpu.get_barrier_semaphore()
    greeted = [(zs[0], ys[o]) for o in range(1, gy)]
    greeted += [(zs[o], ys[j]) for o in (1, gz - 1) for j in range(gy)]
    greeted += [(zs[o], ys[0]) for o in range(2, gz - 1)]
    for device in greeted:
        pl.semaphore_signal(barrier, inc=1, device_id=device, device_id_type=MESH)

    y_rows = pl.ds(pl.multiple_of(my_y * y_len, y_len), y_len)
    for b in range(own):
        grain, phase = grains[b * BLOCK], phases[b * BLOCK]

        def pick_class(i, cls):
            return jnp.where(grain == i, grain_class[i], cls)

        cls = lax.fori_loop(0, grain_class.shape[0], pick_class, jnp.zeros_like(grain))
        kappa = jnp.zeros(grain.shape, jnp.float32)
        for p in range(diffusivity.shape[0]):
            for c in range(diffusivity.shape[1]):
                kappa = jnp.where((phase == p) & (cls == c), diffusivity[p, c], kappa)
        k_all[1 + SIDE + b, y_rows] = kappa
    c_all[pl.ds(halo, z_len), y_rows] = conc[...]

    pl.semaphore_wait(barrier, len(greeted))

    sends = []

    def send(src, dst, send_sem, recv_sem, device):
        copy = pltpu.make_async_remote_copy(
            src_ref=src, dst_ref=dst, send_sem=send_sem, recv_sem=recv_sem,
            device_id=device, device_id_type=MESH,
        )
        copy.start()
        sends.append(copy)
        return copy

    first_round = []
    plans = [(zs[0], o, 0, z_len, halo) for o in range(1, gy)]
    plans += [(zs[1], o, z_len - halo, halo, 0) for o in range(gy)]
    plans += [(zs[gz - 1], o, 0, halo, halo + z_len) for o in range(gy)]
    for n, (z, o, start, length, to) in enumerate(plans):
        first_round.append(send(
            k_all.at[pl.ds(1 + SIDE + start // BLOCK, length // BLOCK), y_rows],
            k_all.at[pl.ds(1 + to // BLOCK, length // BLOCK), y_rows],
            k_send.at[n], k_recv.at[n], (z, ys[o]),
        ))
    fields = []
    for n, (z, o, start, length, to) in enumerate(plans):
        fields.append(send(
            conc.at[pl.ds(start, length)],
            c_all.at[pl.ds(to, length), y_rows],
            c_send.at[n], c_recv.at[n], (z, ys[o]),
        ))

    for copy in first_round:
        copy.wait_recv()
    k_all[0:1] = k_all[1:2]
    k_all[blocks + 1 : blocks + 2] = k_all[blocks : blocks + 1]

    z2_rows = pl.ds(own * my_z, own)
    z2_rows_padded = pl.ds(1 + own * my_z, own)
    for b in range(own):
        k2[1 + own * my_z + b] = (
            k_all.at[1 + SIDE + b][pl.ds(0, y2, stride=BLOCK), :] * 0.25
        )
    second_round = [
        send(
            k2.at[z2_rows_padded], k2.at[z2_rows_padded],
            k2_send.at[o - 1], k2_recv.at[o - 1], (zs[o], ys[0]),
        )
        for o in range(1, gz)
    ]

    u2 = 8
    l0 = Level(f0, k_all, 1.0, blocks, 4, 1, 1, 1, False)
    l1 = Level(f1, k_all, 0.5, blocks, 2, 1, 2, 2, False)
    l2 = Level(f2, k2, 1.0, nz2, 1, u2, 1, 4, True)
    l3 = Level(f3, k3, 1.0, nz2 // 2, 1, u2, 2, 8, True)
    l4 = Level(f4, k4, 1.0, nz2 // 4, 1, u2, 4, 16, True)
    l0.build()
    l1.build()
    for copy in fields:
        copy.wait_recv()

    for cycle in range(CYCLES):
        if cycle == 0:
            l0.first(va, c_all)
        else:
            l0.relax(va, vn, c_all)
        l0.relax(vb, va, c_all)
        l0.restrict(g1, vb, c_all)
        l1.first(v1a, g1)
        l1.relax(v1b, v1a, g1)

        def own_rest(b):
            rest[pl.ds(b - SIDE, 1)] = l1.restricted(v1b, g1, b)

        l1.loop(own_rest, SIDE, SIDE + own)
        source2 = g2.at[cycle]
        for b in range(own):
            source2[own * my_z + b] = rest.at[b][pl.ds(0, y2, stride=BLOCK), :]
        gathered = [
            send(
                source2.at[z2_rows], source2.at[z2_rows],
                g2_send.at[cycle, o - 1], g2_recv.at[cycle, o - 1], (zs[o], ys[0]),
            )
            for o in range(1, gz)
        ]
        if cycle == 0:
            for copy in second_round:
                copy.wait_recv()
            l2.ghosts(k2)
            l2.build()
            for fine, coarse, level in ((k2, k3, l2), (k3, k4, l3)):

                def coarser(b):
                    coarse[pl.ds(b // 2 + 1, u2 // 2)] = (
                        block_sum(fine[pl.ds(b + 1, u2)], level.sy, level.sx) * 0.0625
                    )

                level.loop(coarser)
                above = l3 if level is l2 else l4
                above.ghosts(coarse)
                above.build()
        for copy in gathered:
            copy.wait_recv()

        l2.first(v2a, source2)
        l2.relax(v2b, v2a, source2)
        l2.restrict(g3, v2b, source2)
        l3.first(v3a, g3)
        l3.relax(v3b, v3a, g3)
        l3.restrict(g4, v3b, g3)
        l4.first(v4a, g4)
        here, there = v4a, v4b
        for _ in range(COARSE - 1):
            l4.relax(there, here, g4)
            here, there = there, here
        l3.correct(v3b, here)
        l3.relax(v3a, v3b, g3)
        l3.relax(v3b, v3a, g3)
        l2.correct(v2b, v3b)
        l2.relax(v2a, v2b, source2)
        l2.relax(v2b, v2a, source2)

        def widen(b):
            z = lax.rem(own * my_z + b - SIDE + nz2, nz2)
            value = v2b[z + 1]
            target = spread.at[b + 1]
            for k in range(BLOCK):
                target[pl.ds(k, y2, stride=BLOCK), :] = value

        l1.loop(widen, 1, blocks - 1)
        l1.correct(v1b, spread, 1, blocks - 1)
        l1.relax(v1a, v1b, g1, 1, blocks - 1)
        l1.relax(v1b, v1a, g1, 1, blocks - 1)
        l0.correct(vb, v1b, 2, blocks - 2)
        l0.relax(va, vb, c_all, 2, blocks - 2)
        if cycle < CYCLES - 1:
            l0.relax(vn, va, c_all, SIDE, SIDE + own)
            halves = [
                send(
                    vn.at[pl.ds(1 + z_len, halo)], vn.at[pl.ds(1, halo)],
                    v_send.at[0], v_recv.at[0], (zs[1], ys[0]),
                ),
                send(
                    vn.at[pl.ds(1 + halo, halo)], vn.at[pl.ds(1 + halo + z_len, halo)],
                    v_send.at[1], v_recv.at[1], (zs[gz - 1], ys[0]),
                ),
            ]
            for copy in halves:
                copy.wait_recv()
        else:
            l0.relax(vb, va, c_all, SIDE, SIDE + own)
    out[...] = vb[pl.ds(1 + halo, z_len), y_rows]

    for copy in sends:
        copy.wait_send()


def per_device(gz, gy, concentration, phases, grains, grain_class, diffusivity):
    z_len, y_len, x_len = concentration.shape
    blocks = z_len // BLOCK + 2 * SIDE
    y_all = y_len * gy
    y2 = y_all // BLOCK
    nz2 = z_len // BLOCK * gz
    z_all = blocks * BLOCK
    near = 3 * gy - 1

    def vmem(*shape):
        return pltpu.VMEM(shape + (x_len,), jnp.float32)

    def sems(*shape):
        return pltpu.SemaphoreType.DMA(shape)

    scratch = [
        vmem(z_all, y_all), vmem(blocks + 2, y_all),
        vmem(z_all + 2, y_all), vmem(z_all + 2, y_all), vmem(z_all + 2, y_all),
        vmem(z_all // 2, y_all), vmem(z_all // 2 + 2, y_all), vmem(z_all // 2 + 2, y_all),
        vmem(z_len // BLOCK, y_all), vmem(blocks + 2, y_all),
        vmem(nz2 + 2, y2), vmem(CYCLES, nz2, y2), vmem(nz2 + 2, y2), vmem(nz2 + 2, y2),
    ]
    for rows in (nz2 // 2, nz2 // 4):
        scratch += [vmem(rows + 2, y2), vmem(rows, y2), vmem(rows + 2, y2), vmem(rows + 2, y2)]
    scratch += [vmem(10, blocks, y_all), vmem(10, blocks, y_all)]
    scratch += [vmem(8, rows, y2) for rows in (nz2, nz2 // 2, nz2 // 4)]
    scratch += [sems(near)] * 4 + [sems(gz - 1)] * 2 + [sems(CYCLES, gz - 1)] * 2 + [sems(2)] * 2
    in_vmem = pl.BlockSpec(memory_space=pltpu.VMEM)
    in_smem = pl.BlockSpec(memory_space=pltpu.SMEM)
    return pl.pallas_call(
        functools.partial(kernel, gz, gy),
        out_shape=jax.ShapeDtypeStruct(concentration.shape, jnp.float32),
        in_specs=[in_vmem, in_vmem, in_vmem, in_smem, in_smem],
        out_specs=in_vmem,
        scratch_shapes=scratch,
        compiler_params=pltpu.CompilerParams(
            collective_id=0, has_side_effects=True, vmem_limit_bytes=40 * 1024 * 1024
        ),
    )(concentration, phases, grains, grain_class, diffusivity)


def solution(mesh):
    placed = (P("gz", "gy", None), P("gz", "gy", None), P("gz", "gy", None), P(), P())
    body = functools.partial(per_device, mesh.shape["gz"], mesh.shape["gy"])
    return jax.shard_map(
        body, mesh=mesh, in_specs=placed, out_specs=P("gz", "gy", None), check_vma=False
    )
```

```python
import functools

import jax
import jax.numpy as jnp
from jax import lax
from jax.experimental import pallas as pl
from jax.experimental.pallas import tpu as pltpu
from jax.sharding import PartitionSpec as P

CYCLES = 2
COARSE = 6
RELAX_WEIGHT = 0.8
KEEP = 1.0 - RELAX_WEIGHT
BLOCK = 4
SIDE = 3
MESH = pl.DeviceIdType.MESH

XL, XH, YL, YH, ZL, ZH, KI, W0, WM, WL = range(10)


def roll(values, shift, axis):
    return pltpu.roll(values, shift % values.shape[axis], axis)


def harmonic(near_k, far_k):
    return 2.0 * near_k * far_k / (near_k + far_k)


def pair_sum(values, stride, axis):
    index = lax.broadcasted_iota(jnp.int32, values.shape, axis)
    odd = (index & stride) != 0
    other = jnp.where(odd, roll(values, stride, axis), roll(values, -stride, axis))
    return values + other


def block_sum(values, sy, sx):
    rows = values.shape[0]
    halved = jnp.concatenate(
        [values[j : j + 1] + values[j + 1 : j + 2] for j in range(0, rows, 2)], axis=0
    )
    return pair_sum(pair_sum(halved, sy, 1), sx, 2)


def doubled(values):
    rows = values.shape[0]
    return jnp.concatenate([values[j // 2 : j // 2 + 1] for j in range(2 * rows)], axis=0)


class Level:
    def __init__(self, faces, kappa, scale, blocks, rpb, u, sy, sx, periodic):
        self.faces, self.kappa, self.scale = faces, kappa, scale
        self.blocks, self.rpb, self.u = blocks, rpb, u
        self.sy, self.sx, self.periodic = sy, sx, periodic

    def loop(self, body, low=0, high=None):
        high = self.blocks if high is None else high

        def step(i, carry):
            body(low + i * self.u)
            return carry

        lax.fori_loop(0, (high - low) // self.u, step, 0)

    def ghosts(self, ref):
        if self.periodic:
            rows = self.blocks * self.rpb
            ref[0:1] = ref[rows : rows + 1]
            ref[rows + 1 : rows + 2] = ref[1:2]

    def build(self):
        faces, rpb, u = self.faces, self.rpb, self.u

        def body(b):
            k = self.kappa[pl.ds(b + 1, u)] * self.scale
            below = self.kappa[pl.ds(b, u)] * self.scale
            above = self.kappa[pl.ds(b + 2, u)] * self.scale
            row = lax.broadcasted_iota(jnp.int32, k.shape, 1)
            col = lax.broadcasted_iota(jnp.int32, k.shape, 2)
            y_size, x_size = k.shape[1], k.shape[2]
            sy, sx = self.sy, self.sx
            xl = jnp.where(col < sx, 0.0, harmonic(k, roll(k, sx, 2)))
            xh = jnp.where(col >= x_size - sx, 0.0, harmonic(k, roll(k, -sx, 2)))
            yl = jnp.where(row < sy, 0.0, harmonic(k, roll(k, sy, 1)))
            yh = jnp.where(row >= y_size - sy, 0.0, harmonic(k, roll(k, -sy, 1)))
            zl = harmonic(k, below)
            zh = harmonic(k, above)
            base = 1.0 + xl + xh + yl + yh
            at = pl.ds(b, u)
            for name, value in ((XL, xl), (XH, xh), (YL, yl), (YH, yh), (ZL, zl), (ZH, zh), (KI, k)):
                faces[name, at] = value
            if rpb == 1:
                faces[W0, at] = RELAX_WEIGHT / (base + zl + zh)
            else:
                faces[W0, at] = RELAX_WEIGHT / (base + zl + k)
                faces[WL, at] = RELAX_WEIGHT / (base + zh + k)
                if rpb > 2:
                    faces[WM, at] = RELAX_WEIGHT / (base + k + k)

        self.loop(body)

    def weight(self, b):
        if self.rpb == 1:
            return self.faces[W0, pl.ds(b, self.u)]
        parts = []
        for j in range(self.u):
            at = pl.ds(b + j, 1)
            middle = [self.faces[WM, at]] * (self.rpb - 2) if self.rpb > 2 else []
            parts += [self.faces[W0, at], *middle, self.faces[WL, at]]
        return jnp.concatenate(parts, axis=0)

    def face(self, name, b):
        if self.rpb == 1 or self.u == 1:
            return self.faces[name, pl.ds(b, self.u)]
        parts = []
        for j in range(self.u):
            parts += [self.faces[name, pl.ds(b + j, 1)]] * self.rpb
        return jnp.concatenate(parts, axis=0)

    def z_faces(self, b):
        at = pl.ds(b, self.u)
        if self.rpb == 1:
            return self.faces[ZL, at], self.faces[ZH, at]
        low, high = [], []
        for j in range(self.u):
            at = pl.ds(b + j, 1)
            inner = [self.faces[KI, at]] * (self.rpb - 1)
            low += [self.faces[ZL, at], *inner]
            high += [*inner, self.faces[ZH, at]]
        return jnp.concatenate(low, axis=0), jnp.concatenate(high, axis=0)

    def terms(self, src, b):
        n = self.u * self.rpb
        ext = src[pl.ds(b * self.rpb, n + 2)]
        centre = ext[1 : n + 1]
        low, high = self.z_faces(b)
        pairs = [
            (low, ext[:n]),
            (high, ext[2:]),
            (self.face(YL, b), roll(centre, self.sy, 1)),
            (self.face(YH, b), roll(centre, -self.sy, 1)),
            (self.face(XL, b), roll(centre, self.sx, 2)),
            (self.face(XH, b), roll(centre, -self.sx, 2)),
        ]
        return centre, pairs

    def rows(self, b, shift=0):
        return pl.ds(b * self.rpb + shift, self.u * self.rpb)

    def first(self, dst, source):
        def body(b):
            dst[self.rows(b, 1)] = self.weight(b) * source[self.rows(b)]

        self.loop(body)
        self.ghosts(dst)

    def relax(self, dst, src, source, low=0, high=None):
        def body(b):
            centre, pairs = self.terms(src, b)
            total = source[self.rows(b)]
            for face, value in pairs:
                total = total + face * value
            dst[self.rows(b, 1)] = KEEP * centre + self.weight(b) * total

        self.loop(body, low, high)
        self.ghosts(dst)

    def restricted(self, src, source, b):
        centre, pairs = self.terms(src, b)
        rest = source[self.rows(b)] - centre
        for face, value in pairs:
            rest = rest - face * (centre - value)
        return block_sum(rest, self.sy, self.sx) * 0.125

    def restrict(self, dst, src, source, low=0, high=None):
        half = self.u * self.rpb // 2

        def body(b):
            dst[pl.ds(b * self.rpb // 2, half)] = self.restricted(src, source, b)

        self.loop(body, low, high)

    def correct(self, dst, coarse, low=0, high=None):
        half = self.u * self.rpb // 2

        def body(b):
            fine = self.rows(b, 1)
            dst[fine] = dst[fine] + doubled(coarse[pl.ds(b * self.rpb // 2 + 1, half)])

        self.loop(body, low, high)
        self.ghosts(dst)


def kernel(
    gz, gy, conc, phases, grains, grain_class, diffusivity, out,
    c_all, k_all, va, vb, vn, g1, v1a, v1b, rest, spread,
    k2, g2, v2a, v2b, k3, g3, v3a, v3b, k4, g4, v4a, v4b, f0, f1, f2, f3, f4,
    c_send, c_recv, k_send, k_recv, k2_send, k2_recv, g2_send, g2_recv, v_send, v_recv,
    in_sem, grain_in, phase_in,
):
    my_z, my_y = lax.axis_index("gz"), lax.axis_index("gy")
    z_len, y_len = conc.shape[0], conc.shape[1]
    own = z_len // BLOCK
    blocks = own + 2 * SIDE
    halo = SIDE * BLOCK
    nz2 = k2.shape[0] - 2
    y2 = k2.shape[1]
    zs = [lax.rem(my_z + o, gz) for o in range(gz)]
    ys = [lax.rem(my_y + o, gy) for o in range(gy)]

    barrier = pltpu.get_barrier_semaphore()
    greeted = [(zs[0], ys[o]) for o in range(1, gy)]
    greeted += [(zs[o], ys[j]) for o in (1, gz - 1) for j in range(gy)]
    greeted += [(zs[o], ys[0]) for o in range(2, gz - 1)]
    for device in greeted:
        pl.semaphore_signal(barrier, inc=1, device_id=device, device_id_type=MESH)

    y_rows = pl.ds(pl.multiple_of(my_y * y_len, y_len), y_len)
    loads = [
        pltpu.make_async_copy(conc, c_all.at[pl.ds(halo, z_len), y_rows], in_sem.at[0]),
    ]
    for b in range(own):
        loads += [
            pltpu.make_async_copy(grains.at[b * BLOCK], grain_in.at[b], in_sem.at[1 + 2 * b]),
            pltpu.make_async_copy(phases.at[b * BLOCK], phase_in.at[b], in_sem.at[2 + 2 * b]),
        ]
    for copy in loads:
        copy.start()
    for copy in loads:
        copy.wait()
    grain, phase = grain_in[...], phase_in[...]
    cls = jnp.zeros_like(grain)
    for i in range(grain_class.shape[0]):
        cls = jnp.where(grain == i, grain_class[i], cls)
    classes = diffusivity.shape[1]
    label = phase * classes + cls
    kappa = jnp.zeros(grain.shape, jnp.float32)
    for p in range(diffusivity.shape[0]):
        for c in range(classes):
            kappa = jnp.where(label == p * classes + c, diffusivity[p, c], kappa)
    k_all[pl.ds(1 + SIDE, own), y_rows] = kappa

    pl.semaphore_wait(barrier, len(greeted))

    sends = []

    def send(src, dst, send_sem, recv_sem, device):
        copy = pltpu.make_async_remote_copy(
            src_ref=src, dst_ref=dst, send_sem=send_sem, recv_sem=recv_sem,
            device_id=device, device_id_type=MESH,
        )
        copy.start()
        sends.append(copy)
        return copy

    first_round = []
    plans = [(zs[0], o, 0, z_len, halo) for o in range(1, gy)]
    plans += [(zs[1], o, z_len - halo, halo, 0) for o in range(gy)]
    plans += [(zs[gz - 1], o, 0, halo, halo + z_len) for o in range(gy)]
    for n, (z, o, start, length, to) in enumerate(plans):
        first_round.append(send(
            k_all.at[pl.ds(1 + SIDE + start // BLOCK, length // BLOCK), y_rows],
            k_all.at[pl.ds(1 + to // BLOCK, length // BLOCK), y_rows],
            k_send.at[n], k_recv.at[n], (z, ys[o]),
        ))
    fields = []
    near = halo - 2
    plans = [(zs[0], o, 0, z_len, halo) for o in range(1, gy)]
    plans += [(zs[1], o, z_len - near, near, halo - near) for o in range(gy)]
    plans += [(zs[gz - 1], o, 0, near, halo + z_len) for o in range(gy)]
    for n, (z, o, start, length, to) in enumerate(plans):
        fields.append(send(
            c_all.at[pl.ds(halo + start, length), y_rows],
            c_all.at[pl.ds(to, length), y_rows],
            c_send.at[n], c_recv.at[n], (z, ys[o]),
        ))

    for copy in first_round:
        copy.wait_recv()
    k_all[0:1] = k_all[1:2]
    k_all[blocks + 1 : blocks + 2] = k_all[blocks : blocks + 1]

    z2_rows = pl.ds(own * my_z, own)
    z2_rows_padded = pl.ds(1 + own * my_z, own)
    for b in range(own):
        k2[1 + own * my_z + b] = (
            k_all.at[1 + SIDE + b][pl.ds(0, y2, stride=BLOCK), :] * 0.25
        )
    second_round = [
        send(
            k2.at[z2_rows_padded], k2.at[z2_rows_padded],
            k2_send.at[o - 1], k2_recv.at[o - 1], (zs[o], ys[0]),
        )
        for o in range(1, gz)
    ]

    u2, u3, u4 = [min(16, nz2 // m) for m in (1, 2, 4)]
    l0 = Level(f0, k_all, 1.0, blocks, 4, 1, 1, 1, False)
    l1 = Level(f1, k_all, 0.5, blocks, 2, 2, 2, 2, False)
    l2 = Level(f2, k2, 1.0, nz2, 1, u2, 1, 4, True)
    l3 = Level(f3, k3, 1.0, nz2 // 2, 1, u3, 2, 8, True)
    l4 = Level(f4, k4, 1.0, nz2 // 4, 1, u4, 4, 16, True)
    l0.build()
    l1.build()
    for copy in fields:
        copy.wait_recv()

    for cycle in range(CYCLES):
        if cycle == 0:
            l0.first(va, c_all)
        else:
            l0.relax(va, vn, c_all)
        l0.relax(vb, va, c_all)
        l0.restrict(g1, vb, c_all)
        l1.first(v1a, g1)
        l1.relax(v1b, v1a, g1)

        def own_rest(b):
            rest[pl.ds(b - SIDE, l1.u)] = l1.restricted(v1b, g1, b)

        l1.loop(own_rest, SIDE, SIDE + own)
        source2 = g2.at[cycle]
        for b in range(own):
            source2[own * my_z + b] = rest.at[b][pl.ds(0, y2, stride=BLOCK), :]
        gathered = [
            send(
                source2.at[z2_rows], source2.at[z2_rows],
                g2_send.at[cycle, o - 1], g2_recv.at[cycle, o - 1], (zs[o], ys[0]),
            )
            for o in range(1, gz)
        ]
        if cycle == 0:
            for copy in second_round:
                copy.wait_recv()
            l2.ghosts(k2)
            l2.build()
            for fine, coarse, level in ((k2, k3, l2), (k3, k4, l3)):

                def coarser(b):
                    coarse[pl.ds(b // 2 + 1, level.u // 2)] = (
                        block_sum(fine[pl.ds(b + 1, level.u)], level.sy, level.sx) * 0.0625
                    )

                level.loop(coarser)
                above = l3 if level is l2 else l4
                above.ghosts(coarse)
                above.build()
        for copy in gathered:
            copy.wait_recv()

        l2.first(v2a, source2)
        l2.relax(v2b, v2a, source2)
        l2.restrict(g3, v2b, source2)
        l3.first(v3a, g3)
        l3.relax(v3b, v3a, g3)
        l3.restrict(g4, v3b, g3)
        l4.first(v4a, g4)
        here, there = v4a, v4b
        for _ in range(COARSE - 1):
            l4.relax(there, here, g4)
            here, there = there, here
        l3.correct(v3b, here)
        l3.relax(v3a, v3b, g3)
        l3.relax(v3b, v3a, g3)
        l2.correct(v2b, v3b)
        l2.relax(v2a, v2b, source2)
        l2.relax(v2b, v2a, source2)

        for b in range(1, blocks - 1):
            z = lax.rem(own * my_z + b - SIDE + nz2, nz2)
            value = v2b[z + 1]
            target = spread.at[b + 1]
            for k in range(BLOCK):
                target[pl.ds(k, y2, stride=BLOCK), :] = value

        l1.correct(v1b, spread, 1, blocks - 1)
        l1.relax(v1a, v1b, g1, 1, blocks - 1)
        l1.relax(v1b, v1a, g1, 1, blocks - 1)
        l0.correct(vb, v1b, 2, blocks - 2)
        l0.relax(va, vb, c_all, 2, blocks - 2)
        if cycle < CYCLES - 1:
            l0.relax(vn, va, c_all, SIDE, SIDE + own)
            halves = [
                send(
                    vn.at[pl.ds(2 + z_len, halo - 1)], vn.at[pl.ds(2, halo - 1)],
                    v_send.at[0], v_recv.at[0], (zs[1], ys[0]),
                ),
                send(
                    vn.at[pl.ds(1 + halo, halo - 1)],
                    vn.at[pl.ds(1 + halo + z_len, halo - 1)],
                    v_send.at[1], v_recv.at[1], (zs[gz - 1], ys[0]),
                ),
            ]
            for copy in halves:
                copy.wait_recv()
        else:
            l0.relax(vb, va, c_all, SIDE, SIDE + own)
    out[...] = vb[pl.ds(1 + halo, z_len), y_rows]

    for copy in sends:
        copy.wait_send()


def per_device(gz, gy, concentration, phases, grains, grain_class, diffusivity):
    z_len, y_len, x_len = concentration.shape
    blocks = z_len // BLOCK + 2 * SIDE
    y_all = y_len * gy
    y2 = y_all // BLOCK
    nz2 = z_len // BLOCK * gz
    z_all = blocks * BLOCK
    near = 3 * gy - 1

    def vmem(*shape):
        return pltpu.VMEM(shape + (x_len,), jnp.float32)

    def sems(*shape):
        return pltpu.SemaphoreType.DMA(shape)

    scratch = [
        vmem(z_all, y_all), vmem(blocks + 2, y_all),
        vmem(z_all + 2, y_all), vmem(z_all + 2, y_all), vmem(z_all + 2, y_all),
        vmem(z_all // 2, y_all), vmem(z_all // 2 + 2, y_all), vmem(z_all // 2 + 2, y_all),
        vmem(z_len // BLOCK, y_all), vmem(blocks + 2, y_all),
        vmem(nz2 + 2, y2), vmem(CYCLES, nz2, y2), vmem(nz2 + 2, y2), vmem(nz2 + 2, y2),
    ]
    for rows in (nz2 // 2, nz2 // 4):
        scratch += [vmem(rows + 2, y2), vmem(rows, y2), vmem(rows + 2, y2), vmem(rows + 2, y2)]
    scratch += [vmem(10, blocks, y_all), vmem(10, blocks, y_all)]
    scratch += [vmem(8, rows, y2) for rows in (nz2, nz2 // 2, nz2 // 4)]
    scratch += [sems(near)] * 4 + [sems(gz - 1)] * 2 + [sems(CYCLES, gz - 1)] * 2 + [sems(2)] * 2
    planes = (z_len // BLOCK, y_len, x_len)
    scratch += [sems(1 + 2 * planes[0])] + [pltpu.VMEM(planes, jnp.int32)] * 2
    in_hbm = pl.BlockSpec(memory_space=pl.ANY)
    in_vmem = pl.BlockSpec(memory_space=pltpu.VMEM)
    in_smem = pl.BlockSpec(memory_space=pltpu.SMEM)
    return pl.pallas_call(
        functools.partial(kernel, gz, gy),
        out_shape=jax.ShapeDtypeStruct(concentration.shape, jnp.float32),
        in_specs=[in_hbm, in_hbm, in_hbm, in_smem, in_smem],
        out_specs=in_vmem,
        scratch_shapes=scratch,
        compiler_params=pltpu.CompilerParams(
            collective_id=0, has_side_effects=True, vmem_limit_bytes=60 * 1024 * 1024
        ),
    )(concentration, phases, grains, grain_class, diffusivity)


def solution(mesh):
    placed = (P("gz", "gy", None), P("gz", "gy", None), P("gz", "gy", None), P(), P())
    body = functools.partial(per_device, mesh.shape["gz"], mesh.shape["gy"])
    return jax.shard_map(
        body, mesh=mesh, in_specs=placed, out_specs=P("gz", "gy", None), check_vma=False
    )
```

```python
import functools

import jax
import jax.numpy as jnp
from jax import lax
from jax.experimental import pallas as pl
from jax.experimental.pallas import tpu as pltpu
from jax.sharding import PartitionSpec as P

CYCLES = 2
COARSE = 6
RELAX_WEIGHT = 0.8
KEEP = 1.0 - RELAX_WEIGHT
BLOCK = 4
SIDE = 3
MESH = pl.DeviceIdType.MESH

XL, XH, YL, YH, ZL, ZH, KI, W0, WM, WL = range(10)


def roll(values, shift, axis):
    return pltpu.roll(values, shift % values.shape[axis], axis)


def harmonic(near_k, far_k):
    return 2.0 * near_k * far_k / (near_k + far_k)


def pair_sum(values, stride, axis):
    index = lax.broadcasted_iota(jnp.int32, values.shape, axis)
    odd = (index & stride) != 0
    other = jnp.where(odd, roll(values, stride, axis), roll(values, -stride, axis))
    return values + other


def block_sum(values, sy, sx):
    rows = values.shape[0]
    halved = jnp.concatenate(
        [values[j : j + 1] + values[j + 1 : j + 2] for j in range(0, rows, 2)], axis=0
    )
    return pair_sum(pair_sum(halved, sy, 1), sx, 2)


def doubled(values):
    rows = values.shape[0]
    return jnp.concatenate([values[j // 2 : j // 2 + 1] for j in range(2 * rows)], axis=0)


def pack(rows):
    col = lax.broadcasted_iota(jnp.int32, rows[0].shape, 1) & (BLOCK - 1)
    packed = rows[0]
    for b in range(1, len(rows)):
        packed = jnp.where(col == b, rows[b], packed)
    return packed


def unpack(dst, packed, count, shift):
    col = lax.broadcasted_iota(jnp.int32, packed.shape, 2) & (BLOCK - 1)
    for b in range(count):
        lanes = jnp.where(col == b, packed, 0.0)
        values = pair_sum(pair_sum(lanes, 1, 2), 2, 2)
        for d in range(packed.shape[0]):
            dst[d * count + b + shift] = values[d]


class Level:
    def __init__(self, faces, kappa, scale, blocks, rpb, u, sy, sx, periodic):
        self.faces, self.kappa, self.scale = faces, kappa, scale
        self.blocks, self.rpb, self.u = blocks, rpb, u
        self.sy, self.sx, self.periodic = sy, sx, periodic

    def loop(self, body, low=0, high=None):
        high = self.blocks if high is None else high

        def step(i, carry):
            body(low + i * self.u)
            return carry

        lax.fori_loop(0, (high - low) // self.u, step, 0)

    def ghosts(self, ref):
        if self.periodic:
            rows = self.blocks * self.rpb
            ref[0:1] = ref[rows : rows + 1]
            ref[rows + 1 : rows + 2] = ref[1:2]

    def build(self):
        faces, rpb, u = self.faces, self.rpb, self.u

        def body(b):
            k = self.kappa[pl.ds(b + 1, u)] * self.scale
            below = self.kappa[pl.ds(b, u)] * self.scale
            above = self.kappa[pl.ds(b + 2, u)] * self.scale
            row = lax.broadcasted_iota(jnp.int32, k.shape, 1)
            col = lax.broadcasted_iota(jnp.int32, k.shape, 2)
            y_size, x_size = k.shape[1], k.shape[2]
            sy, sx = self.sy, self.sx
            xl = jnp.where(col < sx, 0.0, harmonic(k, roll(k, sx, 2)))
            xh = jnp.where(col >= x_size - sx, 0.0, harmonic(k, roll(k, -sx, 2)))
            yl = jnp.where(row < sy, 0.0, harmonic(k, roll(k, sy, 1)))
            yh = jnp.where(row >= y_size - sy, 0.0, harmonic(k, roll(k, -sy, 1)))
            zl = harmonic(k, below)
            zh = harmonic(k, above)
            base = 1.0 + xl + xh + yl + yh
            at = pl.ds(b, u)
            for name, value in ((XL, xl), (XH, xh), (YL, yl), (YH, yh), (ZL, zl), (ZH, zh), (KI, k)):
                faces[name, at] = value
            if rpb == 1:
                faces[W0, at] = RELAX_WEIGHT / (base + zl + zh)
            else:
                faces[W0, at] = RELAX_WEIGHT / (base + zl + k)
                faces[WL, at] = RELAX_WEIGHT / (base + zh + k)
                if rpb > 2:
                    faces[WM, at] = RELAX_WEIGHT / (base + k + k)

        self.loop(body)

    def weight(self, b):
        if self.rpb == 1:
            return self.faces[W0, pl.ds(b, self.u)]
        parts = []
        for j in range(self.u):
            at = pl.ds(b + j, 1)
            middle = [self.faces[WM, at]] * (self.rpb - 2) if self.rpb > 2 else []
            parts += [self.faces[W0, at], *middle, self.faces[WL, at]]
        return jnp.concatenate(parts, axis=0)

    def face(self, name, b):
        if self.rpb == 1 or self.u == 1:
            return self.faces[name, pl.ds(b, self.u)]
        parts = []
        for j in range(self.u):
            parts += [self.faces[name, pl.ds(b + j, 1)]] * self.rpb
        return jnp.concatenate(parts, axis=0)

    def z_faces(self, b):
        at = pl.ds(b, self.u)
        if self.rpb == 1:
            return self.faces[ZL, at], self.faces[ZH, at]
        low, high = [], []
        for j in range(self.u):
            at = pl.ds(b + j, 1)
            inner = [self.faces[KI, at]] * (self.rpb - 1)
            low += [self.faces[ZL, at], *inner]
            high += [*inner, self.faces[ZH, at]]
        return jnp.concatenate(low, axis=0), jnp.concatenate(high, axis=0)

    def terms(self, src, b):
        n = self.u * self.rpb
        ext = src[pl.ds(b * self.rpb, n + 2)]
        centre = ext[1 : n + 1]
        low, high = self.z_faces(b)
        pairs = [
            (low, ext[:n]),
            (high, ext[2:]),
            (self.face(YL, b), roll(centre, self.sy, 1)),
            (self.face(YH, b), roll(centre, -self.sy, 1)),
            (self.face(XL, b), roll(centre, self.sx, 2)),
            (self.face(XH, b), roll(centre, -self.sx, 2)),
        ]
        return centre, pairs

    def rows(self, b, shift=0):
        return pl.ds(b * self.rpb + shift, self.u * self.rpb)

    def first(self, dst, source):
        def body(b):
            dst[self.rows(b, 1)] = self.weight(b) * source[self.rows(b)]

        self.loop(body)
        self.ghosts(dst)

    def relax(self, dst, src, source, low=0, high=None):
        def body(b):
            centre, pairs = self.terms(src, b)
            total = source[self.rows(b)]
            for face, value in pairs:
                total = total + face * value
            dst[self.rows(b, 1)] = KEEP * centre + self.weight(b) * total

        self.loop(body, low, high)
        self.ghosts(dst)

    def restricted(self, src, source, b):
        centre, pairs = self.terms(src, b)
        rest = source[self.rows(b)] - centre
        for face, value in pairs:
            rest = rest - face * (centre - value)
        return block_sum(rest, self.sy, self.sx) * 0.125

    def restrict(self, dst, src, source, low=0, high=None):
        half = self.u * self.rpb // 2

        def body(b):
            dst[pl.ds(b * self.rpb // 2, half)] = self.restricted(src, source, b)

        self.loop(body, low, high)

    def correct(self, dst, coarse, low=0, high=None):
        half = self.u * self.rpb // 2

        def body(b):
            fine = self.rows(b, 1)
            dst[fine] = dst[fine] + doubled(coarse[pl.ds(b * self.rpb // 2 + 1, half)])

        self.loop(body, low, high)
        self.ghosts(dst)


def kernel(
    gz, gy, conc, phases, grains, grain_class, diffusivity, out,
    c_all, k_all, va, vb, vn, g1, v1a, v1b, rest, spread,
    k2, g2, v2a, v2b, k3, g3, v3a, v3b, k4, g4, v4a, v4b, f0, f1, f2, f3, f4,
    c_send, c_recv, k_send, k_recv, k2_send, k2_recv, g2_send, g2_recv, v_send, v_recv,
    in_sem, grain_in, phase_in, k2_packed, g2_packed,
):
    my_z, my_y = lax.axis_index("gz"), lax.axis_index("gy")
    z_len, y_len = conc.shape[0], conc.shape[1]
    own = z_len // BLOCK
    blocks = own + 2 * SIDE
    halo = SIDE * BLOCK
    nz2 = k2.shape[0] - 2
    y2 = k2.shape[1]
    zs = [lax.rem(my_z + o, gz) for o in range(gz)]
    ys = [lax.rem(my_y + o, gy) for o in range(gy)]

    barrier = pltpu.get_barrier_semaphore()
    greeted = [(zs[0], ys[o]) for o in range(1, gy)]
    greeted += [(zs[o], ys[j]) for o in (1, gz - 1) for j in range(gy)]
    greeted += [(zs[o], ys[0]) for o in range(2, gz - 1)]
    for device in greeted:
        pl.semaphore_signal(barrier, inc=1, device_id=device, device_id_type=MESH)

    y_rows = pl.ds(pl.multiple_of(my_y * y_len, y_len), y_len)
    loads = [
        pltpu.make_async_copy(conc, c_all.at[pl.ds(halo, z_len), y_rows], in_sem.at[0]),
    ]
    for b in range(own):
        loads += [
            pltpu.make_async_copy(grains.at[b * BLOCK], grain_in.at[b], in_sem.at[1 + 2 * b]),
            pltpu.make_async_copy(phases.at[b * BLOCK], phase_in.at[b], in_sem.at[2 + 2 * b]),
        ]
    for copy in loads:
        copy.start()
    for copy in loads:
        copy.wait()
    grain, phase = grain_in[...], phase_in[...]
    cls = jnp.zeros_like(grain)
    for i in range(grain_class.shape[0]):
        cls = jnp.where(grain == i, grain_class[i], cls)
    classes = diffusivity.shape[1]
    label = phase * classes + cls
    kappa = jnp.zeros(grain.shape, jnp.float32)
    for p in range(diffusivity.shape[0]):
        for c in range(classes):
            kappa = jnp.where(label == p * classes + c, diffusivity[p, c], kappa)
    k_all[pl.ds(1 + SIDE, own), y_rows] = kappa

    pl.semaphore_wait(barrier, len(greeted))

    sends = []

    def send(src, dst, send_sem, recv_sem, device):
        copy = pltpu.make_async_remote_copy(
            src_ref=src, dst_ref=dst, send_sem=send_sem, recv_sem=recv_sem,
            device_id=device, device_id_type=MESH,
        )
        copy.start()
        sends.append(copy)
        return copy

    first_round = []
    plans = [(zs[0], o, 0, z_len, halo) for o in range(1, gy)]
    plans += [(zs[1], o, z_len - halo, halo, 0) for o in range(gy)]
    plans += [(zs[gz - 1], o, 0, halo, halo + z_len) for o in range(gy)]
    for n, (z, o, start, length, to) in enumerate(plans):
        first_round.append(send(
            k_all.at[pl.ds(1 + SIDE + start // BLOCK, length // BLOCK), y_rows],
            k_all.at[pl.ds(1 + to // BLOCK, length // BLOCK), y_rows],
            k_send.at[n], k_recv.at[n], (z, ys[o]),
        ))
    core = lax.rem(my_y, 2)
    sibling = my_y + 1 - 2 * core
    near = halo - 2
    fields = [send(
        c_all.at[pl.ds(halo, z_len), y_rows], c_all.at[pl.ds(halo, z_len), y_rows],
        c_send.at[0], c_recv.at[0], (zs[0], sibling),
    )]
    direct = []
    spans = [(0, 0, z_len, halo), (1, z_len - near, near, halo - near), (gz - 1, 0, near, halo + z_len)]
    for dz, start, length, to in spans:
        for o in range(0, gy, 2):
            if dz == 0 and o == 0:
                continue
            n = 1 + len(direct)
            copy = send(
                c_all.at[pl.ds(halo + start, length), y_rows],
                c_all.at[pl.ds(to, length), y_rows],
                c_send.at[n], c_recv.at[n], (zs[dz], ys[o]),
            )
            came_y = pl.ds(pl.multiple_of(ys[(gy - o) % gy] * y_len, y_len), y_len)
            direct.append((copy, c_all.at[pl.ds(to, length), came_y]))

    for copy in first_round:
        copy.wait_recv()
    k_all[0:1] = k_all[1:2]
    k_all[blocks + 1 : blocks + 2] = k_all[blocks : blocks + 1]

    k2_packed[my_z] = pack(
        [k_all.at[1 + SIDE + b][pl.ds(0, y2, stride=BLOCK), :] * 0.25 for b in range(own)]
    )
    second_round = [
        send(
            k2_packed.at[my_z], k2_packed.at[my_z],
            k2_send.at[o - 1], k2_recv.at[o - 1], (zs[o], ys[0]),
        )
        for o in range(1, gz)
    ]

    u2, u3, u4 = [min(16, nz2 // m) for m in (1, 2, 4)]
    l0 = Level(f0, k_all, 1.0, blocks, 4, 1, 1, 1, False)
    l1 = Level(f1, k_all, 0.5, blocks, 2, 2, 2, 2, False)
    l2 = Level(f2, k2, 1.0, nz2, 1, u2, 1, 4, True)
    l3 = Level(f3, k3, 1.0, nz2 // 2, 1, u3, 2, 8, True)
    l4 = Level(f4, k4, 1.0, nz2 // 4, 1, u4, 4, 16, True)
    l0.build()
    for n, (copy, came) in enumerate(direct):
        copy.wait_recv()
        m = 1 + len(direct) + n
        fields.append(send(came, came, c_send.at[m], c_recv.at[m], (zs[0], sibling)))
    l1.build()
    for copy in fields:
        copy.wait_recv()

    for cycle in range(CYCLES):
        if cycle == 0:
            l0.first(va, c_all)
        else:
            l0.relax(va, vn, c_all)
        l0.relax(vb, va, c_all)
        l0.restrict(g1, vb, c_all)
        l1.first(v1a, g1)
        l1.relax(v1b, v1a, g1)

        def own_rest(b):
            rest[pl.ds(b - SIDE, l1.u)] = l1.restricted(v1b, g1, b)

        l1.loop(own_rest, SIDE, SIDE + own)
        source2 = g2
        mine = g2_packed.at[cycle, my_z]
        mine[...] = pack([rest.at[b][pl.ds(0, y2, stride=BLOCK), :] for b in range(own)])
        gathered = [
            send(
                mine, mine,
                g2_send.at[cycle, o - 1], g2_recv.at[cycle, o - 1], (zs[o], ys[0]),
            )
            for o in range(1, gz)
        ]
        if cycle == 0:
            for copy in second_round:
                copy.wait_recv()
            unpack(k2, k2_packed[...], own, 1)
            l2.ghosts(k2)
            l2.build()
            for fine, coarse, level in ((k2, k3, l2), (k3, k4, l3)):

                def coarser(b):
                    coarse[pl.ds(b // 2 + 1, level.u // 2)] = (
                        block_sum(fine[pl.ds(b + 1, level.u)], level.sy, level.sx) * 0.0625
                    )

                level.loop(coarser)
                above = l3 if level is l2 else l4
                above.ghosts(coarse)
                above.build()
        for copy in gathered:
            copy.wait_recv()
        unpack(g2, g2_packed[cycle], own, 0)

        l2.first(v2a, source2)
        l2.relax(v2b, v2a, source2)
        l2.restrict(g3, v2b, source2)
        l3.first(v3a, g3)
        l3.relax(v3b, v3a, g3)
        l3.restrict(g4, v3b, g3)
        l4.first(v4a, g4)
        here, there = v4a, v4b
        for _ in range(COARSE - 1):
            l4.relax(there, here, g4)
            here, there = there, here
        l3.correct(v3b, here)
        l3.relax(v3a, v3b, g3)
        l3.relax(v3b, v3a, g3)
        l2.correct(v2b, v3b)
        l2.relax(v2a, v2b, source2)
        l2.relax(v2b, v2a, source2)

        for b in range(1, blocks - 1):
            z = lax.rem(own * my_z + b - SIDE + nz2, nz2)
            value = v2b[z + 1]
            target = spread.at[b + 1]
            for k in range(BLOCK):
                target[pl.ds(k, y2, stride=BLOCK), :] = value

        l1.correct(v1b, spread, 1, blocks - 1)
        l1.relax(v1a, v1b, g1, 1, blocks - 1)
        l1.relax(v1b, v1a, g1, 1, blocks - 1)
        l0.correct(vb, v1b, 2, blocks - 2)
        l0.relax(va, vb, c_all, 2, blocks - 2)
        if cycle < CYCLES - 1:
            l0.relax(vn, va, c_all, SIDE, SIDE + own)
            y_half = conc.shape[1] * gy // 2
            half = pl.ds(pl.multiple_of(core * y_half, y_half), y_half)
            sides = []
            for n, (dz, start, to) in enumerate(
                ((1, 2 + z_len, 2), (gz - 1, 1 + halo, 1 + halo + z_len))
            ):
                came = vn.at[pl.ds(to, halo - 1), half]
                sides.append((n, came, send(
                    vn.at[pl.ds(start, halo - 1), half], came,
                    v_send.at[n], v_recv.at[n], (zs[dz], ys[0]),
                )))
            relays = []
            for n, came, copy in sides:
                copy.wait_recv()
                relays.append(send(
                    came, came, v_send.at[2 + n], v_recv.at[2 + n], (zs[0], sibling)
                ))
            for copy in relays:
                copy.wait_recv()
        else:
            l0.relax(vb, va, c_all, SIDE, SIDE + own)
    out[...] = vb[pl.ds(1 + halo, z_len), y_rows]

    for copy in sends:
        copy.wait_send()


def per_device(gz, gy, concentration, phases, grains, grain_class, diffusivity):
    z_len, y_len, x_len = concentration.shape
    blocks = z_len // BLOCK + 2 * SIDE
    y_all = y_len * gy
    y2 = y_all // BLOCK
    nz2 = z_len // BLOCK * gz
    z_all = blocks * BLOCK
    near = 3 * gy - 1
    assert z_len // BLOCK == BLOCK and gy % 2 == 0

    def vmem(*shape):
        return pltpu.VMEM(shape + (x_len,), jnp.float32)

    def sems(*shape):
        return pltpu.SemaphoreType.DMA(shape)

    scratch = [
        vmem(z_all, y_all), vmem(blocks + 2, y_all),
        vmem(z_all + 2, y_all), vmem(z_all + 2, y_all), vmem(z_all + 2, y_all),
        vmem(z_all // 2, y_all), vmem(z_all // 2 + 2, y_all), vmem(z_all // 2 + 2, y_all),
        vmem(z_len // BLOCK, y_all), vmem(blocks + 2, y_all),
        vmem(nz2 + 2, y2), vmem(nz2, y2), vmem(nz2 + 2, y2), vmem(nz2 + 2, y2),
    ]
    for rows in (nz2 // 2, nz2 // 4):
        scratch += [vmem(rows + 2, y2), vmem(rows, y2), vmem(rows + 2, y2), vmem(rows + 2, y2)]
    scratch += [vmem(10, blocks, y_all), vmem(10, blocks, y_all)]
    scratch += [vmem(8, rows, y2) for rows in (nz2, nz2 // 2, nz2 // 4)]
    scratch += [sems(near)] * 4 + [sems(gz - 1)] * 2 + [sems(CYCLES, gz - 1)] * 2 + [sems(4)] * 2
    planes = (z_len // BLOCK, y_len, x_len)
    scratch += [sems(1 + 2 * planes[0])] + [pltpu.VMEM(planes, jnp.int32)] * 2
    scratch += [vmem(gz, y2), vmem(CYCLES, gz, y2)]
    in_hbm = pl.BlockSpec(memory_space=pl.ANY)
    in_vmem = pl.BlockSpec(memory_space=pltpu.VMEM)
    in_smem = pl.BlockSpec(memory_space=pltpu.SMEM)
    return pl.pallas_call(
        functools.partial(kernel, gz, gy),
        out_shape=jax.ShapeDtypeStruct(concentration.shape, jnp.float32),
        in_specs=[in_hbm, in_hbm, in_hbm, in_smem, in_smem],
        out_specs=in_vmem,
        scratch_shapes=scratch,
        compiler_params=pltpu.CompilerParams(
            collective_id=0, has_side_effects=True, vmem_limit_bytes=60 * 1024 * 1024
        ),
    )(concentration, phases, grains, grain_class, diffusivity)


def solution(mesh):
    placed = (P("gz", "gy", None), P("gz", "gy", None), P("gz", "gy", None), P(), P())
    body = functools.partial(per_device, mesh.shape["gz"], mesh.shape["gy"])
    return jax.shard_map(
        body, mesh=mesh, in_specs=placed, out_specs=P("gz", "gy", None), check_vma=False
    )
```
